256 devices in a mesh: group: 16 (over x, y), member: 8 (over z), half: 2 (over core).
Axes of the slice: x: 4, y: 4, z: 8, core: 2. Of those that a mesh axis runs over, the one named last changes fastest.
Arguments:
- tokens: bfloat16 [16384, 2048], P(('group', 'member'), 'half'), may hold values from -6 to 6
- group_ids: int32 [16384, 1], P(('group', 'member')), may hold values from 0 to 15, as said below
- expert_ids: int32 [2, 16384, 4], P(None, ('group', 'member')), may hold values from 0 to 7, as said below
- gate_weights: bfloat16 [2, 16384, 4], P(None, ('group', 'member')), may hold values from 0.25 to 1
- w_gate: bfloat16 [128, 2048, 768], P(('group', 'member'), None, 'half'), may hold values from -0.125 to 0.125
- w_up: bfloat16 [128, 2048, 768], P(('group', 'member'), None, 'half'), may hold values from -0.125 to 0.125
- w_down: bfloat16 [128, 768, 2048], P(('group', 'member'), 'half'), may hold values from -0.21875 to 0.21875
Outputs:
- rows_out: bfloat16 [16384, 2048], P(('group', 'member'), 'half')
The draws below stay inside these ranges and needn't reach their ends.
Inputs may be any that keep to these rules, and one draw needn't show every extreme that they name: `group_ids`: in each aligned block of 128 rows (the rows of one device) at most 12 rows name the same group, and in every block some group is named by exactly 12 rows. `expert_ids`: each row names four different members. Among the rows of one device that name one group, in one pass, at most 6 name the same member; the rows of one device that take up all 12 slots of a group reach it. Every member is named by some row.
All inputs are finite; a program needn't handle non-finite values.
Results may differ from the reference program's by a relative error of at most 0.015.
Values may be sent and summed in bfloat16 or wider, within the bound.
A program may use at most 64 MiB of HBM per device.

```python
import jax
import jax.numpy as jnp
from jax import lax

D = 2048
FF = 768
TOK_DEV = 128
PASSES = 2
EXPERTS = 128
TOKENS = 16384
CAP_G = 12
N_GROUP = 16
N_MEMBER = 8
N_HALF = 2


def routing(key):
    base = jax.random.fold_in(key, 7301)
    block_count = N_GROUP * N_MEMBER
    slot_total = N_GROUP * CAP_G
    key_hot, key_bias, key_score, key_order, key_perm = jax.random.split(base, 5)
    hot_member = jax.random.randint(key_hot, (N_MEMBER,), 0, N_GROUP)
    hot_block = jnp.tile(hot_member, N_GROUP)
    bias = jax.random.randint(key_bias, (N_GROUP,), 0, 4)
    label = jnp.arange(slot_total, dtype=jnp.int32) // CAP_G
    noise = jax.random.randint(key_score, (block_count, slot_total), 0, 1024)
    score = noise + bias[label][None, :] * 1024 + (label[None, :] == hot_block[:, None]).astype(jnp.int32) * 8192
    score = score * slot_total + jnp.arange(slot_total, dtype=jnp.int32)[None, :]
    unused, chosen = lax.top_k(score, TOK_DEV)
    order = jax.random.randint(key_order, (block_count, TOK_DEV), 0, 1 << 20) * TOK_DEV + jnp.arange(TOK_DEV, dtype=jnp.int32)[None, :]
    shuffle = jnp.argsort(order, axis=1)
    chosen = jnp.take_along_axis(chosen, shuffle, axis=1)
    groups = (chosen // CAP_G).astype(jnp.int32)
    onehot = (groups[:, :, None] == jnp.arange(N_GROUP, dtype=jnp.int32)[None, None, :]).astype(jnp.int32)
    before = jnp.cumsum(onehot, axis=1) - onehot
    ranking = jnp.sum(before * onehot, axis=2)
    perm_score = jax.random.randint(key_perm, (PASSES, block_count, N_GROUP, N_MEMBER), 0, 1 << 20) * N_MEMBER + jnp.arange(N_MEMBER, dtype=jnp.int32)
    members_perm = jnp.argsort(perm_score, axis=3).astype(jnp.int32)
    index = jnp.broadcast_to(groups[None, :, :, None], (PASSES, block_count, TOK_DEV, N_MEMBER))
    token_perm = jnp.take_along_axis(members_perm, index, axis=2)
    window = (4 * ranking[:, :, None] + jnp.arange(4, dtype=jnp.int32)[None, None, :]) % N_MEMBER
    window = jnp.broadcast_to(window[None], (PASSES, block_count, TOK_DEV, 4))
    picks = jnp.take_along_axis(token_perm, window, axis=3)
    return (groups.reshape(TOKENS, 1), picks.reshape(PASSES, TOKENS, 4).astype(jnp.int32))


def draw_group_ids(key, part):
    return routing(key)[0]


def draw_expert_ids(key, part):
    return routing(key)[1]


def levels(stream_key, dims, cuts, smallest, top_value):
    factor_of, own = 1.0, jax.random.fold_in(stream_key, 6)
    for dim, parts in cuts:
        steps = jnp.exp(jax.random.uniform(jax.random.fold_in(own, dim), (parts,), jnp.float32, smallest / len(cuts), top_value / len(cuts)))
        factor_of = factor_of * jnp.repeat(steps, dims[dim] // parts).reshape([-1 if axis == dim else 1 for axis in range(len(dims))])
    return factor_of


def gaussian(own_key, dims, width, reach, cuts=(), held_as=jnp.bfloat16):
    values = jax.random.normal(own_key, dims, jnp.float32) * width
    if len(cuts) > 0:
        values = levels(own_key, dims, cuts, -0.22, 0.18) * values
    return jnp.clip(values, min=-reach, max=reach).astype(held_as)


def setup_inputs(seed: int = 0) -> dict:
    splits = jax.random.split(jax.random.key(seed), 8)
    tokens = gaussian(splits[0], (TOKENS, D), 1.0, 6.0, ((0, 128), (1, 2)))
    group_ids = draw_group_ids(jax.random.fold_in(splits[7], 71), 0)
    expert_ids = draw_expert_ids(jax.random.fold_in(splits[7], 71), 0)
    gate_weights = jnp.clip(0.25 + 0.75 * jax.random.uniform(splits[3], (PASSES, TOKENS, 4), jnp.float32) ** levels(splits[3], (PASSES, TOKENS, 4), ((1, 128),), -0.2, 0.2), 0.25, 1.0).astype(jnp.bfloat16)
    w_gate = gaussian(splits[4], (EXPERTS, D, FF), D ** -0.5, 0.125, ((0, 128), (2, 2)))
    w_up = gaussian(splits[5], (EXPERTS, D, FF), D ** -0.5, 0.125, ((0, 128), (2, 2)))
    w_down = gaussian(splits[6], (EXPERTS, FF, D), FF ** -0.5, 0.21875, ((0, 128), (1, 2)))
    return dict(tokens=tokens, group_ids=group_ids, expert_ids=expert_ids, gate_weights=gate_weights, w_gate=w_gate, w_up=w_up, w_down=w_down)


epsilon = 1e-06

def expert_terms(rows, gates, weight_gate, weight_up, weight_down):
    pre_gate = jnp.dot(rows, weight_gate, preferred_element_type=jnp.float32)
    up_value = jnp.dot(rows, weight_up, preferred_element_type=jnp.float32)
    hidden = (jax.nn.silu(pre_gate) * up_value).astype(jnp.bfloat16)
    hidden_split = hidden.reshape(rows.shape[0], N_HALF, FF // N_HALF).astype(jnp.float32)
    down_split = weight_down.reshape(N_HALF, FF // N_HALF, D).astype(jnp.float32)
    halves_out = jnp.einsum('rhf,hfd->hrd', hidden_split, down_split)
    rounded = (halves_out * gates[None, :, None]).astype(jnp.bfloat16)
    rounded = lax.optimization_barrier(rounded)
    return lax.optimization_barrier(jnp.sum(rounded.astype(jnp.float32), axis=0))

def group_pass(rows, table, gate_all, up_all, down_all):

    def add_expert(carry, pieces):
        weight_gate, weight_up, weight_down, column = pieces
        return (carry + expert_terms(rows, column, weight_gate, weight_up, weight_down), None)
    start_total = jnp.zeros((rows.shape[0], D), jnp.float32)
    totals, unused = lax.scan(add_expert, start_total, (gate_all, up_all, down_all, table.T))
    lifted = rows.astype(jnp.float32) + totals
    factor = lax.rsqrt(lax.optimization_barrier(jnp.mean(lifted * lifted, axis=1, keepdims=True)) + epsilon)
    return (lifted * factor).astype(jnp.bfloat16)

def reference(tokens, group_ids, expert_ids, gate_weights, w_gate, w_up, w_down):
    token_count = tokens.shape[0]
    slot_count = N_GROUP * CAP_G
    group_rows = N_MEMBER * slot_count
    route_group = group_ids[:, 0].astype(jnp.int32)
    anchor = jnp.arange(token_count, dtype=jnp.int32) // TOK_DEV
    from_group = anchor // N_MEMBER
    from_member = anchor % N_MEMBER
    onehot = (route_group[:, None] == jnp.arange(N_GROUP, dtype=jnp.int32)[None, :]).astype(jnp.int32)
    blocks = onehot.reshape(-1, TOK_DEV, N_GROUP)
    before = (jnp.cumsum(blocks, axis=1) - blocks).reshape(token_count, N_GROUP)
    ranking = lax.optimization_barrier(jnp.sum(before * onehot, axis=1))
    position = (from_member * slot_count + from_group * CAP_G + ranking).astype(jnp.int32)
    stream = jnp.zeros((N_GROUP, group_rows, D), jnp.bfloat16).at[route_group, position].set(tokens)
    member_ids = jnp.arange(N_MEMBER, dtype=jnp.int32)
    dense_gates = lax.optimization_barrier(jnp.sum(gate_weights.astype(jnp.float32)[..., None] * (expert_ids[..., None] == member_ids).astype(jnp.float32), axis=2))
    gate_table = jnp.zeros((PASSES, N_GROUP, group_rows, N_MEMBER), jnp.float32).at[:, route_group, position].set(dense_gates)
    gates_all = w_gate.reshape(N_GROUP, N_MEMBER, D, FF)
    ups_all = w_up.reshape(N_GROUP, N_MEMBER, D, FF)
    downs_all = w_down.reshape(N_GROUP, N_MEMBER, FF, D)
    for pass_index in range(PASSES):
        stream = lax.map(lambda pieces: group_pass(*pieces), (stream, gate_table[pass_index], gates_all, ups_all, downs_all))
    return stream[route_group, position]
```

```python
import functools

import jax
import jax.numpy as jnp
from jax import lax
from jax.experimental import pallas as pl
from jax.experimental.pallas import tpu as pltpu
from jax.sharding import PartitionSpec as P

MESH = pl.DeviceIdType.MESH
BF16 = jnp.bfloat16
F32 = jnp.float32
EPSILON = 1e-6
SUBS = 4
PICKS = 6
TILE = 8
TILES = 3


def first_rows(value):
    return value[0:8]


def turned_dot(left, right):
    return lax.dot_general(left, right, (((0,), (0,)), ((), ())), preferred_element_type=F32)


def kernel(
    tok_ref, gid_ref, eid_ref, gw_ref, wg_hbm, wu_hbm, wd_hbm, out_ref,
    wg, wu, wd, xa, sel, rows_in, part_out, part_in, acc, term_out, term_in, yv, ring_out, ring_in,
    meta_out, meta, lift, sq_out, sq_in,
    w_sem, g_send, g_recv, r_send, r_recv, x_send, x_recv, t_send, t_recv, d_send, d_recv, p_send, p_recv,
    n_send, n_recv, m_send, m_recv,
):
    g = lax.axis_index("group")
    m = lax.axis_index("member")
    h = lax.axis_index("half")
    groups, members = 16, 8
    rows, width = tok_ref.shape
    sub_rows = rows // SUBS

    def place(group=None, member=None, half=None):
        return (
            g if group is None else group,
            m if member is None else member,
            h if half is None else half,
        )

    above = place(member=lax.rem(m + 1, members))
    below = place(member=lax.rem(m + members - 1, members))
    sibling = place(half=1 - h)
    ring_to = (above, below)

    def send(src, dst, send_sem, recv_sem, target):
        return pltpu.make_async_remote_copy(
            src_ref=src, dst_ref=dst, send_sem=send_sem, recv_sem=recv_sem,
            device_id=target, device_id_type=MESH,
        )

    barrier = pltpu.get_barrier_semaphore()

    def greet(target):
        pl.semaphore_signal(barrier, inc=1, device_id=target, device_id_type=MESH)

    greet(sibling)

    def greet_member(d, c):
        greet(place(member=lax.rem(m + d, members)))
        return c

    def greet_group(d, c):
        greet(place(group=lax.rem(g + d, groups)))
        return c

    lax.fori_loop(1, members, greet_member, 0)
    lax.fori_loop(1, groups, greet_group, 0)

    own_k = pl.ds(pl.multiple_of(h * width, width), width)
    other_k = pl.ds(pl.multiple_of((1 - h) * width, width), width)
    weight_copies = [
        pltpu.make_async_copy(wg_hbm.at[0, own_k, :], wg.at[0], w_sem.at[0]),
        pltpu.make_async_copy(wg_hbm.at[0, other_k, :], wg.at[1], w_sem.at[1]),
        pltpu.make_async_copy(wu_hbm.at[0, own_k, :], wu.at[0], w_sem.at[2]),
        pltpu.make_async_copy(wu_hbm.at[0, other_k, :], wu.at[1], w_sem.at[3]),
        pltpu.make_async_copy(wd_hbm.at[0, :, own_k], wd.at[0], w_sem.at[4]),
        pltpu.make_async_copy(wd_hbm.at[0, :, other_k], wd.at[1], w_sem.at[5]),
    ]
    for copy in weight_copies:
        copy.start()

    lane = lax.broadcasted_iota(jnp.int32, (rows, rows), 1)
    down = lax.broadcasted_iota(jnp.int32, (rows, rows), 0)

    def kind(s):
        return lax.rem(m + s, 2)

    def own(s):
        return kind(s) == 0

    def other(s):
        return kind(s) == 1

    def half_subs(way):
        return range(SUBS // 2) if way == 0 else range(SUBS // 2, SUBS)

    def sub_ds(sub):
        return pl.ds(sub * sub_rows, sub_rows)

    def g_copy(p, s, way, msg, sub):
        pi = kind(s)
        if way == 0:
            src, dst = ((0, pi), (1 + pi, 2 + pi))[msg]
        else:
            src, dst = ((pi, 1 + pi), (2 + pi, 3))[msg]
        sp = 2 * p + s
        return send(
            xa.at[p, s, src, sub_ds(sub)], xa.at[p, s, dst, sub_ds(sub)],
            g_send.at[sp, way, msg, sub], g_recv.at[sp, way, msg, sub], ring_to[way],
        )

    def g_wait(p, s, way, msg, sub):
        pi = kind(s)
        if way == 0:
            dst = (1 - pi, 3 - pi)[msg]
        else:
            dst = (2 - pi, 3)[msg]
        sp = 2 * p + s
        pltpu.make_async_copy(
            xa.at[p, s, dst, sub_ds(sub)], xa.at[p, s, dst, sub_ds(sub)], g_recv.at[sp, way, msg, sub]
        ).wait()

    def gather_own(p, s):
        @pl.when(own(s))
        def _():
            for sub in range(SUBS):
                for way in (0, 1):
                    g_copy(p, s, way, 0, sub).start()

    def gather_first(p, s):
        for sub in range(SUBS):
            for way in (0, 1):
                g_wait(p, s, way, 0, sub)

                @pl.when(own(s))
                def _():
                    g_copy(p, s, way, 1, sub).start()

                @pl.when(other(s))
                def _():
                    g_copy(p, s, way, 0, sub).start()

    def gather_second(p, s):
        @pl.when(own(s))
        def _():
            for way in (0, 1):
                for sub in half_subs(way):
                    g_wait(p, s, way, 1, sub)

        @pl.when(other(s))
        def _():
            for i in range(SUBS):
                for way in (0, 1):
                    sub = i if way == 0 else SUBS - 1 - i
                    g_wait(p, s, way, 1, sub)
                    if sub in half_subs(way):
                        g_copy(p, s, way, 1, sub).start()

    def source(s, j):
        pi = kind(s)
        step = (-pi, 3 * pi - 2, 2 - 5 * pi, 4 - pi)[j]
        return lax.rem(m + members + step, members)

    def matches(p, s, k, j):
        record = meta[source(s, j)]
        code = record[p : p + 1, :].astype(jnp.int32)
        gate = record[2 + p : 3 + p, :]
        off = PICKS * j - TILE * k
        at = (code & 7) + off
        good = (code >= 0) & (at >= 0) & (at < TILE)
        return down == jnp.where(good, code + off, -1), gate

    def choose(p, s, k):
        total = None
        for j in (k, k + 1):
            hit, _ = matches(p, s, k, j)
            piece = jnp.dot(
                jnp.where(hit, 1.0, 0.0).astype(BF16), xa[p, s, j], preferred_element_type=F32
            )
            total = piece if total is None else total + piece
        sp = 2 * p + s
        sel[sp, k] = total.astype(BF16).reshape(groups, TILE, width)
        rows_in[sp, k, 0, pl.ds(g, 1)] = sel[sp, k, pl.ds(g, 1)]

        def start(d, c):
            t = lax.rem(g + d, groups)
            send(
                sel.at[sp, k, t], rows_in.at[sp, k, 0, g], x_send.at[sp, k], x_recv.at[sp, k],
                place(group=t),
            ).start()
            return c

        lax.fori_loop(1, groups, start, 0)

    def most(ref, sem):
        part = ref.at[pl.ds(0, groups - 1)]
        pltpu.make_async_copy(part, part, sem).wait()

    def row_copy(p, s, k):
        sp = 2 * p + s
        return send(
            rows_in.at[sp, k, 0], rows_in.at[sp, k, 1], d_send.at[sp, k], d_recv.at[sp, k], sibling
        )

    def landed(p, s, k):
        sp = 2 * p + s
        most(rows_in.at[sp, k, 0], x_recv.at[sp, k])
        row_copy(p, s, k).start()

    def part_copy(p, s, k):
        sp = 2 * p + s
        return send(
            part_out.at[sp, k], part_in.at[sp, k], p_send.at[sp, k], p_recv.at[sp, k], sibling
        )

    def expert(p, s, k):
        sp = 2 * p + s
        row_copy(p, s, k).wait_recv()
        mine = rows_in[sp, k, 0].reshape(rows, width)
        theirs = rows_in[sp, k, 1].reshape(rows, width)
        pre = jnp.dot(mine, wg[0], preferred_element_type=F32)
        pre += jnp.dot(theirs, wg[1], preferred_element_type=F32)
        up = jnp.dot(mine, wu[0], preferred_element_type=F32)
        up += jnp.dot(theirs, wu[1], preferred_element_type=F32)
        hidden = (jax.nn.silu(pre) * up).astype(BF16)
        part_out[sp, k] = jnp.dot(hidden, wd[1], preferred_element_type=F32).astype(BF16)
        part_copy(p, s, k).start()
        acc[k] = jnp.dot(hidden, wd[0], preferred_element_type=F32)

    def give_back(p, s, k):
        sp = 2 * p + s
        part_copy(p, s, k).wait_recv()
        total = acc[k] + part_in[sp, k].astype(F32)
        term_out[sp, k] = total.astype(BF16).reshape(groups, TILE, width)
        term_in[sp, k, pl.ds(g, 1)] = term_out[sp, k, pl.ds(g, 1)]

        def start(d, c):
            t = lax.rem(g + d, groups)
            send(
                term_out.at[sp, k, t], term_in.at[sp, k, g], t_send.at[sp, k], t_recv.at[sp, k],
                place(group=t),
            ).start()
            return c

        lax.fori_loop(1, groups, start, 0)

    def returned(p, s, k):
        sp = 2 * p + s
        most(term_in.at[sp, k], t_recv.at[sp, k])

    def weigh(p, s, j):
        sp = 2 * p + s
        total = None
        for k in (j - 1, j):
            if 0 <= k < TILES:
                hit, gate = matches(p, s, k, j)
                piece = turned_dot(
                    jnp.where(hit, gate, 0.0).astype(BF16), term_in[sp, k].reshape(rows, width)
                )
                total = piece if total is None else total + piece
        yv[s, j] = total

    def r_copy(p, s, way, msg, sub):
        sp = 2 * p + s
        return send(
            ring_out.at[sp, way, msg, sub_ds(sub)], ring_in.at[sp, way, msg, sub_ds(sub)],
            r_send.at[sp, way, msg, sub], r_recv.at[sp, way, msg, sub], ring_to[way],
        )

    def sum_start(p, s):
        sp = 2 * p + s

        @pl.when(own(s))
        def _():
            for i in range(SUBS // 2):
                for way in (0, 1):
                    sub = half_subs(way)[i]
                    ring_out[sp, way, 0, sub_ds(sub)] = yv[s, 3, sub_ds(sub)].astype(BF16)
                    r_copy(p, s, way, 0, sub).start()

    def sum_middle(p, s):
        sp = 2 * p + s

        @pl.when(other(s))
        def _():
            order = [(i, way) for i in range(SUBS) for way in (0, 1)]
            fresh = [x for x in order if x[0] not in half_subs(x[1])]
            for sub, way in fresh + [x for x in order if x not in fresh]:
                value = yv[s, (3, 2)[way], sub_ds(sub)]
                if (sub, way) not in fresh:
                    r_copy(p, s, way, 0, sub).wait_recv()
                    value += ring_in[sp, way, 0, sub_ds(sub)].astype(F32)
                ring_out[sp, way, 0, sub_ds(sub)] = value.astype(BF16)
                r_copy(p, s, way, 0, sub).start()

        @pl.when(own(s))
        def _():
            order = [(i, way) for i in range(SUBS) for way in (0, 1)]
            fresh = [x for x in order if x[0] not in half_subs(x[1])]
            for sub, way in fresh + [x for x in order if x not in fresh]:
                r_copy(p, s, way, 0, sub).wait_recv()
                value = yv[s, (2, 1)[way], sub_ds(sub)] + ring_in[sp, way, 0, sub_ds(sub)].astype(F32)
                ring_out[sp, way, 1, sub_ds(sub)] = value.astype(BF16)
                r_copy(p, s, way, 1, sub).start()

    def sum_last(p, s):
        sp = 2 * p + s

        @pl.when(other(s))
        def _():
            order = [(i, way) for i in range(SUBS) for way in (0, 1)]
            fresh = [x for x in order if x[0] not in half_subs(x[1])]
            for sub, way in fresh + [x for x in order if x not in fresh]:
                r_copy(p, s, way, 1, sub).wait_recv()
                value = yv[s, (1, 0)[way], sub_ds(sub)] + ring_in[sp, way, 1, sub_ds(sub)].astype(F32)
                ring_out[sp, way, 1, sub_ds(sub)] = value.astype(BF16)
                r_copy(p, s, way, 1, sub).start()

    def square_copy(p):
        return send(sq_out.at[p], sq_in.at[p], n_send.at[p], n_recv.at[p], sibling)

    def finish(p, s):
        sp = 2 * p + s

        @pl.when(own(s))
        def _():
            for sub in range(SUBS):
                at = sub_ds(sub)
                for way in (0, 1):
                    r_copy(p, s, way, 1, sub).wait_recv()
                value = xa[p, s, 0, at].astype(F32) + yv[s, 0, at]
                value += ring_in[sp, 0, 1, at].astype(F32) + ring_in[sp, 1, 1, at].astype(F32)
                lift[at] = value
                square = value * value
                part = square[:, 0:128]
                for c in range(128, width, 128):
                    part += square[:, c : c + 128]
                sq_out[p, at] = part
            square_copy(p).start()
            square_copy(p).wait_recv()
            for sub in range(SUBS):
                at = sub_ds(sub)
                mean = jnp.sum(sq_out[p, at] + sq_in[p, at], axis=1, keepdims=True) / (2 * width)
                value = (lift[at] * lax.rsqrt(mean + EPSILON)).astype(BF16)
                if p == 0:
                    xa[1, s, 0, at] = value
                else:
                    out_ref[at] = value

    for s in (0, 1):

        @pl.when(own(s))
        def _():
            xa[0, s, 0] = tok_ref[...]

    pl.semaphore_wait(barrier, groups + members - 1)
    gather_own(0, 0)

    group_of = gid_ref[...]
    onehot = jnp.where(group_of == lane, 1.0, 0.0).astype(BF16)
    same = lax.dot_general(onehot, onehot, (((1,), (1,)), ((), ())), preferred_element_type=F32)
    before = jnp.where(down < lane, same, 0.0).astype(BF16)
    eye = jnp.where(down == lane, 1.0, 0.0).astype(BF16)
    group_row = first_rows(
        turned_dot(jnp.broadcast_to(group_of.astype(F32), (rows, rows)).astype(BF16), eye)
    )
    meta_out[...] = jnp.zeros_like(meta_out)
    for p in (0, 1):
        ids = eid_ref[p]
        weights = gw_ref[p].astype(F32)
        named = jnp.zeros((rows, rows), F32)
        gates = jnp.zeros((rows, rows), F32)
        for c in range(ids.shape[1]):
            hit = ids[:, c : c + 1] == lane
            named += jnp.where(hit, 1.0, 0.0)
            gates += jnp.where(hit, weights[:, c : c + 1], 0.0)
        named = named.astype(BF16)
        rank_row = first_rows(turned_dot(named, before))
        named_row = first_rows(turned_dot(named, eye))
        gate_row = first_rows(turned_dot(gates.astype(BF16), eye))
        code_row = jnp.where(named_row > 0.5, group_row * TILE + rank_row, -1.0)
        for e in range(members):
            meta_out[e, p : p + 1, :] = code_row[e : e + 1]
            meta_out[e, 2 + p : 3 + p, :] = gate_row[e : e + 1]
    meta[pl.ds(m, 1)] = meta_out[pl.ds(m, 1)]

    def send_meta(d, c):
        to = lax.rem(m + d, members)
        send(meta_out.at[to], meta.at[m], m_send.at[0], m_recv.at[0], place(member=to)).start()
        return c

    lax.fori_loop(1, members, send_meta, 0)

    def meta_wait(sem):
        part = meta.at[pl.ds(0, members - 1)]
        pltpu.make_async_copy(part, part, sem.at[0]).wait()

    for p in (0, 1):
        gather_first(p, 0)
        gather_own(p, 1)
        if p == 0:
            meta_wait(m_recv)
        choose(p, 0, 0)
        gather_second(p, 0)
        choose(p, 0, 1)
        choose(p, 0, 2)
        landed(p, 0, 0)
        gather_first(p, 1)
        if p == 0:
            for copy in weight_copies:
                copy.wait()
        expert(p, 0, 0)
        landed(p, 0, 1)
        choose(p, 1, 0)
        give_back(p, 0, 0)
        landed(p, 0, 2)
        expert(p, 0, 1)
        gather_second(p, 1)
        choose(p, 1, 1)
        expert(p, 0, 2)
        give_back(p, 0, 1)
        choose(p, 1, 2)
        give_back(p, 0, 2)
        landed(p, 1, 0)
        returned(p, 0, 0)
        returned(p, 0, 1)
        landed(p, 1, 1)
        returned(p, 0, 2)
        weigh(p, 0, 3)
        sum_start(p, 0)
        weigh(p, 0, 2)
        weigh(p, 0, 1)
        expert(p, 1, 0)
        sum_middle(p, 0)
        landed(p, 1, 2)
        weigh(p, 0, 0)
        give_back(p, 1, 0)
        expert(p, 1, 1)
        sum_last(p, 0)
        expert(p, 1, 2)
        give_back(p, 1, 1)
        give_back(p, 1, 2)
        returned(p, 1, 0)
        returned(p, 1, 1)
        returned(p, 1, 2)
        weigh(p, 1, 3)
        sum_start(p, 1)
        weigh(p, 1, 2)
        finish(p, 0)
        if p == 0:
            gather_own(1, 0)
        weigh(p, 1, 1)
        sum_middle(p, 1)
        weigh(p, 1, 0)
        sum_last(p, 1)
        finish(p, 1)

    meta_wait(m_send)
    for p in (0, 1):
        square_copy(p).wait_send()
        for s in (0, 1):
            sp = 2 * p + s
            for k in range(TILES):
                most(sel.at[sp, k], x_send.at[sp, k])
                most(term_out.at[sp, k], t_send.at[sp, k])
                row_copy(p, s, k).wait_send()
                part_copy(p, s, k).wait_send()
            for way in (0, 1):
                for sub in range(SUBS):
                    g_copy(p, s, way, 0, sub).wait_send()
                    r_copy(p, s, way, 1, sub).wait_send()
                    if sub in half_subs(way):
                        g_copy(p, s, way, 1, sub).wait_send()
                        r_copy(p, s, way, 0, sub).wait_send()
                    else:

                        @pl.when(own(s))
                        def _():
                            g_copy(p, s, way, 1, sub).wait_send()

                        @pl.when(other(s))
                        def _():
                            r_copy(p, s, way, 0, sub).wait_send()


def on_device(tokens, group_ids, expert_ids, gate_weights, w_gate, w_up, w_down):
    rows, width = tokens.shape
    hidden = w_gate.shape[2]
    tile = (16, TILE, width)
    block = (rows, width)
    vmem = pl.BlockSpec(memory_space=pltpu.VMEM)
    anywhere = pl.BlockSpec(memory_space=pl.ANY)
    dma = pltpu.SemaphoreType.DMA
    return pl.pallas_call(
        kernel,
        out_shape=jax.ShapeDtypeStruct(block, BF16),
        in_specs=[vmem] * 4 + [anywhere] * 3,
        out_specs=vmem,
        scratch_shapes=[
            pltpu.VMEM((2, width, hidden), BF16),
            pltpu.VMEM((2, width, hidden), BF16),
            pltpu.VMEM((2, hidden, width), BF16),
            pltpu.VMEM((2, 2, 4, *block), BF16),
            pltpu.VMEM((4, TILES, *tile), BF16),
            pltpu.VMEM((4, TILES, 2, *tile), BF16),
            pltpu.VMEM((4, TILES, *block), BF16),
            pltpu.VMEM((4, TILES, *block), BF16),
            pltpu.VMEM((TILES, *block), F32),
            pltpu.VMEM((4, TILES, *tile), BF16),
            pltpu.VMEM((4, TILES, *tile), BF16),
            pltpu.VMEM((2, 4, *block), F32),
            pltpu.VMEM((4, 2, 2, *block), BF16),
            pltpu.VMEM((4, 2, 2, *block), BF16),
            pltpu.VMEM((8, 8, 128), F32),
            pltpu.VMEM((8, 8, 128), F32),
            pltpu.VMEM(block, F32),
            pltpu.VMEM((2, rows, 128), F32),
            pltpu.VMEM((2, rows, 128), F32),
            dma((6,)),
            dma((4, 2, 2, SUBS)),
            dma((4, 2, 2, SUBS)),
            dma((4, 2, 2, SUBS)),
            dma((4, 2, 2, SUBS)),
            dma((4, TILES)),
            dma((4, TILES)),
            dma((4, TILES)),
            dma((4, TILES)),
            dma((4, TILES)),
            dma((4, TILES)),
            dma((4, TILES)),
            dma((4, TILES)),
            dma((2,)),
            dma((2,)),
            dma((1,)),
            dma((1,)),
        ],
        compiler_params=pltpu.CompilerParams(
            collective_id=0, has_side_effects=True, vmem_limit_bytes=60 * 1024 * 1024
        ),
    )(tokens, group_ids, expert_ids, gate_weights, w_gate, w_up, w_down)


def solution(mesh):
    placed = (
        P(("group", "member"), "half"),
        P(("group", "member"), None),
        P(None, ("group", "member"), None),
        P(None, ("group", "member"), None),
        P(("group", "member"), None, "half"),
        P(("group", "member"), None, "half"),
        P(("group", "member"), "half", None),
    )
    return jax.shard_map(
        on_device,
        mesh=mesh,
        in_specs=placed,
        out_specs=P(("group", "member"), "half"),
        check_vma=False,
    )
```

```python
import jax
import jax.numpy as jnp
from jax import lax
from jax.experimental import pallas as pl
from jax.experimental.pallas import tpu as pltpu
from jax.sharding import PartitionSpec as P

MESH = pl.DeviceIdType.MESH
BF16 = jnp.bfloat16
F32 = jnp.float32
EPSILON = 1e-6
TILE = 8
TILES = 6
LAST = TILES - 1
CUTS = 4
BLOCKS = 8
STEP_OF_BLOCK = (0, -1, 1, -2, 2, -3, 3, 4)
FILL = (
    ((0, 0, 0, 4), (1, 4, 4, 8)),
    ((1, -4, 0, 2), (2, 2, 2, 8)),
    ((3, 0, 0, 6), (4, 6, 6, 8)),
    ((4, -2, 0, 4), (5, 4, 4, 8)),
    ((5, -4, 0, 2), (6, 2, 2, 8)),
    ((7, 0, 0, 6), (0, 2, 6, 8)),
)
FAR = ((0, 2), (1, 3))
NEAR = ((1, 3), (0, 2))


def first_rows(value):
    return value[0:8]


def turned_dot(left, right):
    return lax.dot_general(left, right, (((0,), (0,)), ((), ())), preferred_element_type=F32)


def kernel(
    tok_ref, gid_ref, eid_ref, gw_ref, wg_hbm, wu_hbm, wd_hbm, out_ref,
    wg, wu, wd, xa, sel, rows_in, part_out, part_in, acc, term_out, term_in, yv, ring_out, ring_in,
    meta_out, meta, lift, sq_out, sq_in,
    w_sem, g_send, g_recv, r_send, r_recv, x_send, x_recv, t_send, t_recv, d_send, d_recv, p_send, p_recv,
    n_send, n_recv, m_send, m_recv,
):
    g = lax.axis_index("group")
    m = lax.axis_index("member")
    h = lax.axis_index("half")
    groups, members = 16, 8
    rows, width = tok_ref.shape
    cut = width // CUTS

    def place(group=None, member=None, half=None):
        return (
            g if group is None else group,
            m if member is None else member,
            h if half is None else half,
        )

    above = place(member=lax.rem(m + 1, members))
    below = place(member=lax.rem(m + members - 1, members))
    sibling = place(half=1 - h)
    ring_to = (above, below)

    def send(src, dst, send_sem, recv_sem, target):
        return pltpu.make_async_remote_copy(
            src_ref=src, dst_ref=dst, send_sem=send_sem, recv_sem=recv_sem,
            device_id=target, device_id_type=MESH,
        )

    barrier = pltpu.get_barrier_semaphore()

    def greet(target):
        pl.semaphore_signal(barrier, inc=1, device_id=target, device_id_type=MESH)

    greet(sibling)

    def greet_member(d, c):
        greet(place(member=lax.rem(m + d, members)))
        return c

    def greet_group(d, c):
        greet(place(group=lax.rem(g + d, groups)))
        return c

    lax.fori_loop(1, members, greet_member, 0)
    lax.fori_loop(1, groups, greet_group, 0)

    own_k = pl.ds(pl.multiple_of(h * width, width), width)
    other_k = pl.ds(pl.multiple_of((1 - h) * width, width), width)
    weight_copies = [
        pltpu.make_async_copy(wg_hbm.at[0, own_k, :], wg.at[0], w_sem.at[0]),
        pltpu.make_async_copy(wg_hbm.at[0, other_k, :], wg.at[1], w_sem.at[1]),
        pltpu.make_async_copy(wu_hbm.at[0, own_k, :], wu.at[0], w_sem.at[2]),
        pltpu.make_async_copy(wu_hbm.at[0, other_k, :], wu.at[1], w_sem.at[3]),
        pltpu.make_async_copy(wd_hbm.at[0, :, own_k], wd.at[0], w_sem.at[4]),
        pltpu.make_async_copy(wd_hbm.at[0, :, other_k], wd.at[1], w_sem.at[5]),
    ]
    for copy in weight_copies:
        copy.start()

    lane = lax.broadcasted_iota(jnp.int32, (rows, rows), 1)
    down = lax.broadcasted_iota(jnp.int32, (rows, rows), 0)


    def lanes(c):
        return pl.ds(c * cut, cut)

    def g_copy(p, step, way, c):
        src = 0 if step == 1 else 2 * step - 3 + way
        dst = 7 if step == 4 else 2 * step - 1 + way
        return send(
            xa.at[p, src, c], xa.at[p, dst, c],
            g_send.at[p, step - 1, way, c], g_recv.at[p, step - 1, way, c], ring_to[way],
        )

    def gather_start(p):
        for i in range(CUTS):
            for way in (0, 1):
                g_copy(p, 1, way, (FAR[way] + NEAR[way])[i]).start()

    def gather(p, step, which):
        for i in which:
            for way in (0, 1):
                c = (FAR[way] + NEAR[way])[i]
                g_copy(p, step, way, c).wait_recv()
                if step < 3 or (step == 3 and i < 2):
                    g_copy(p, step + 1, way, c).start()

    def matches(p, k, filling):
        j, off, low, high = filling
        record = meta[lax.rem(m + members + STEP_OF_BLOCK[j], members)]
        code = record[p : p + 1, :].astype(jnp.int32)
        gate = record[2 + p : 3 + p, :]
        at = (code & 7) + off
        good = (code >= 0) & (at >= low) & (at < high)
        return down == jnp.where(good, code + off, -1), gate

    def parts_of(k):
        return (0, 1) if k == LAST else (None,)

    def cuts_of(f):
        return range(CUTS) if f is None else range(2 * f, 2 * f + 2)

    def sem_of(f):
        return 0 if f is None else f

    def piece(ref, f):
        return ref if f is None else ref.at[pl.ds(2 * f, 2)]

    def pieces(ref, f):
        return ref if f is None else ref.at[:, pl.ds(2 * f, 2)]

    def choose(p, k, f=None):
        picks = []
        for filling in FILL[k]:
            hit, _ = matches(p, k, filling)
            picks.append((jnp.where(hit, 1.0, 0.0).astype(BF16), filling[0]))
        for c in cuts_of(f):
            total = sum(
                jnp.dot(pick, xa[p, j, c], preferred_element_type=F32) for pick, j in picks
            )
            sel[p, k, :, c] = total.astype(BF16).reshape(groups, TILE, cut)
            rows_in[p, k, 0, pl.ds(g, 1), c] = sel[p, k, pl.ds(g, 1), c]

        def start(d, carry):
            t = lax.rem(g + d, groups)
            send(
                piece(sel.at[p, k, t], f), piece(rows_in.at[p, k, 0, g], f),
                x_send.at[p, k, sem_of(f)], x_recv.at[p, k, sem_of(f)], place(group=t),
            ).start()
            return carry

        lax.fori_loop(1, groups, start, 0)

    def most(ref, sem, f):
        part = ref.at[pl.ds(0, groups - 1)] if f is None else ref.at[pl.ds(0, groups - 1), pl.ds(2 * f, 2)]
        pltpu.make_async_copy(part, part, sem).wait()

    def row_copy(p, k, f=None):
        return send(
            pieces(rows_in.at[p, k, 0], f), pieces(rows_in.at[p, k, 1], f),
            d_send.at[p, k, sem_of(f)], d_recv.at[p, k, sem_of(f)], sibling,
        )

    def landed(p, k, f=None):
        most(rows_in.at[p, k, 0], x_recv.at[p, k, sem_of(f)], f)
        row_copy(p, k, f).start()

    def part_copy(p, k, f=None):
        return send(
            piece(part_out.at[p, k], f), piece(part_in.at[p, k], f),
            p_send.at[p, k, sem_of(f)], p_recv.at[p, k, sem_of(f)], sibling,
        )

    def expert(p, k):
        pre = jnp.zeros((rows, wg.shape[2]), F32)
        up = jnp.zeros((rows, wg.shape[2]), F32)
        for f in parts_of(k):
            row_copy(p, k, f).wait_recv()
            for side in (0, 1):
                for c in cuts_of(f):
                    some = rows_in[p, k, side, :, c].reshape(rows, cut)
                    pre += jnp.dot(some, wg[side, lanes(c), :], preferred_element_type=F32)
                    up += jnp.dot(some, wu[side, lanes(c), :], preferred_element_type=F32)
        hidden = (jax.nn.silu(pre) * up).astype(BF16)
        for f in parts_of(k):
            for c in cuts_of(f):
                part_out[p, k, c] = jnp.dot(
                    hidden, wd[1, :, lanes(c)], preferred_element_type=F32
                ).astype(BF16)
            part_copy(p, k, f).start()
        for c in range(CUTS):
            acc[k, c] = jnp.dot(hidden, wd[0, :, lanes(c)], preferred_element_type=F32)

    def give_back(p, k, f=None):
        part_copy(p, k, f).wait_recv()
        for c in cuts_of(f):
            total = acc[k, c] + part_in[p, k, c].astype(F32)
            term_out[p, k, :, c] = total.astype(BF16).reshape(groups, TILE, cut)
            term_in[p, k, pl.ds(g, 1), c] = term_out[p, k, pl.ds(g, 1), c]

        def start(d, carry):
            t = lax.rem(g + d, groups)
            send(
                piece(term_out.at[p, k, t], f), piece(term_in.at[p, k, g], f),
                t_send.at[p, k, sem_of(f)], t_recv.at[p, k, sem_of(f)], place(group=t),
            ).start()
            return carry

        lax.fori_loop(1, groups, start, 0)

    def returned(p, k, f=None):
        most(term_in.at[p, k], t_recv.at[p, k, sem_of(f)], f)

    def weigh(p, j, f=None):
        picks = []
        for k in range(TILES):
            for filling in FILL[k]:
                if filling[0] == j:
                    hit, gate = matches(p, k, filling)
                    picks.append((jnp.where(hit, gate, 0.0).astype(BF16), k))
        for c in cuts_of(f):
            yv[j, c] = sum(
                turned_dot(pick, term_in[p, k, :, c].reshape(rows, cut)) for pick, k in picks
            )

    def r_copy(p, msg, way, c):
        return send(
            ring_out.at[p, msg, way, c], ring_in.at[p, msg, way, c],
            r_send.at[p, msg, way, c], r_recv.at[p, msg, way, c], ring_to[way],
        )

    def pass_on(p, msg, way, c, add):
        value = yv[7 if msg == 0 else 8 - 2 * msg - way, c]
        if add:
            r_copy(p, msg - 1, way, c).wait_recv()
            value += ring_in[p, msg - 1, way, c].astype(F32)
        ring_out[p, msg, way, c] = value.astype(BF16)
        r_copy(p, msg, way, c).start()

    def sum_far(p, f):
        for way in (0, 1):
            pass_on(p, 0, way, FAR[way][f], False)

    def sum_fresh(p):
        for i in (0, 1):
            for way in (0, 1):
                pass_on(p, 1, way, NEAR[way][i], False)

    def sum_join(p):
        for i in (0, 1):
            for way in (0, 1):
                pass_on(p, 1, way, FAR[way][i], True)

    def sum_on(p, msg):
        for i in range(CUTS):
            for way in (0, 1):
                pass_on(p, msg, way, (NEAR[way] + FAR[way])[i], True)

    def square_copy(p):
        return send(sq_out.at[p], sq_in.at[p], n_send.at[p], n_recv.at[p], sibling)

    def finish(p):
        squares = jnp.zeros((rows, 128), F32)
        for c in (0, 1, 2, 3):
            value = xa[p, 0, c].astype(F32) + yv[0, c]
            for way in (0, 1):
                r_copy(p, 3, way, c).wait_recv()
                value += ring_in[p, 3, way, c].astype(F32)
            lift[c] = value
            square = value * value
            for i in range(0, cut, 128):
                squares += square[:, i : i + 128]
        sq_out[p] = squares
        square_copy(p).start()
        square_copy(p).wait_recv()
        mean = jnp.sum(sq_out[p] + sq_in[p], axis=1, keepdims=True) / (2 * width)
        scale = lax.rsqrt(mean + EPSILON)
        for c in range(CUTS):
            value = (lift[c] * scale).astype(BF16)
            if p == 0:
                xa[1, 0, c] = value
            else:
                out_ref[:, lanes(c)] = value

    for c in range(CUTS):
        xa[0, 0, c] = tok_ref[:, lanes(c)]
    pl.semaphore_wait(barrier, groups + members - 1)
    gather_start(0)

    group_of = gid_ref[...]
    onehot = jnp.where(group_of == lane, 1.0, 0.0).astype(BF16)
    same = lax.dot_general(onehot, onehot, (((1,), (1,)), ((), ())), preferred_element_type=F32)
    before = jnp.where(down < lane, same, 0.0).astype(BF16)
    eye = jnp.where(down == lane, 1.0, 0.0).astype(BF16)
    group_row = first_rows(
        turned_dot(jnp.broadcast_to(group_of.astype(F32), (rows, rows)).astype(BF16), eye)
    )
    meta_out[...] = jnp.zeros_like(meta_out)
    for p in (0, 1):
        ids = eid_ref[p]
        weights = gw_ref[p].astype(F32)
        named = jnp.zeros((rows, rows), F32)
        gates = jnp.zeros((rows, rows), F32)
        for c in range(ids.shape[1]):
            hit = ids[:, c : c + 1] == lane
            named += jnp.where(hit, 1.0, 0.0)
            gates += jnp.where(hit, weights[:, c : c + 1], 0.0)
        named = named.astype(BF16)
        rank_row = first_rows(turned_dot(named, before))
        named_row = first_rows(turned_dot(named, eye))
        gate_row = first_rows(turned_dot(gates.astype(BF16), eye))
        code_row = jnp.where(named_row > 0.5, group_row * TILE + rank_row, -1.0)
        for e in range(members):
            meta_out[e, p : p + 1, :] = code_row[e : e + 1]
            meta_out[e, 2 + p : 3 + p, :] = gate_row[e : e + 1]
    meta[pl.ds(m, 1)] = meta_out[pl.ds(m, 1)]

    def send_meta(d, c):
        to = lax.rem(m + d, members)
        send(meta_out.at[to], meta.at[m], m_send.at[0], m_recv.at[0], place(member=to)).start()
        return c

    lax.fori_loop(1, members, send_meta, 0)

    def meta_wait(sem):
        part = meta.at[pl.ds(0, members - 1)]
        pltpu.make_async_copy(part, part, sem.at[0]).wait()

    for p in (0, 1):
        gather(p, 1, range(CUTS))
        if p == 0:
            meta_wait(m_recv)
        choose(p, 0)
        choose(p, 1)
        gather(p, 2, range(CUTS))
        choose(p, 2)
        landed(p, 0)
        gather(p, 3, (0, 1))
        landed(p, 1)
        if p == 0:
            for copy in weight_copies:
                copy.wait()
        gather(p, 3, (2, 3))
        choose(p, 3)
        choose(p, 4)
        expert(p, 0)
        gather(p, 4, (0,))
        choose(p, LAST, 0)
        gather(p, 4, (1,))
        choose(p, LAST, 1)
        landed(p, 2)
        expert(p, 1)
        expert(p, 2)
        landed(p, 3)
        expert(p, 3)
        give_back(p, 3)
        landed(p, 4)
        expert(p, 4)
        give_back(p, 4)
        landed(p, LAST, 0)
        landed(p, LAST, 1)
        expert(p, LAST)
        give_back(p, LAST, 0)
        give_back(p, LAST, 1)
        give_back(p, 2)
        give_back(p, 1)
        give_back(p, 0)
        returned(p, 3)
        returned(p, 4)
        weigh(p, 6)
        weigh(p, 5)
        sum_fresh(p)
        returned(p, LAST, 0)
        weigh(p, 7, 0)
        sum_far(p, 0)
        returned(p, LAST, 1)
        weigh(p, 7, 1)
        sum_far(p, 1)
        sum_join(p)
        returned(p, 2)
        weigh(p, 4)
        weigh(p, 3)
        sum_on(p, 2)
        returned(p, 1)
        returned(p, 0)
        weigh(p, 2)
        weigh(p, 1)
        weigh(p, 0)
        sum_on(p, 3)
        finish(p)
        if p == 0:
            gather_start(1)

    meta_wait(m_send)
    for p in (0, 1):
        square_copy(p).wait_send()
        for k in range(TILES):
            for f in parts_of(k):
                most(sel.at[p, k], x_send.at[p, k, sem_of(f)], f)
                most(term_out.at[p, k], t_send.at[p, k, sem_of(f)], f)
                row_copy(p, k, f).wait_send()
                part_copy(p, k, f).wait_send()
        for i in range(4):
            for way in (0, 1):
                for c in range(CUTS):
                    if i < 3 or c in FAR[way]:
                        g_copy(p, i + 1, way, c).wait_send()
                        r_copy(p, 3 - i, way, c).wait_send()


def on_device(tokens, group_ids, expert_ids, gate_weights, w_gate, w_up, w_down):
    rows, width = tokens.shape
    hidden = w_gate.shape[2]
    cut = width // CUTS
    tile = (16, CUTS, TILE, cut)
    block = (CUTS, rows, cut)
    vmem = pl.BlockSpec(memory_space=pltpu.VMEM)
    anywhere = pl.BlockSpec(memory_space=pl.ANY)
    dma = pltpu.SemaphoreType.DMA
    return pl.pallas_call(
        kernel,
        out_shape=jax.ShapeDtypeStruct((rows, width), BF16),
        in_specs=[vmem] * 4 + [anywhere] * 3,
        out_specs=vmem,
        scratch_shapes=[
            pltpu.VMEM((2, width, hidden), BF16),
            pltpu.VMEM((2, width, hidden), BF16),
            pltpu.VMEM((2, hidden, width), BF16),
            pltpu.VMEM((2, BLOCKS, *block), BF16),
            pltpu.VMEM((2, TILES, *tile), BF16),
            pltpu.VMEM((2, TILES, 2, *tile), BF16),
            pltpu.VMEM((2, TILES, *block), BF16),
            pltpu.VMEM((2, TILES, *block), BF16),
            pltpu.VMEM((TILES, *block), F32),
            pltpu.VMEM((2, TILES, *tile), BF16),
            pltpu.VMEM((2, TILES, *tile), BF16),
            pltpu.VMEM((BLOCKS, *block), F32),
            pltpu.VMEM((2, 4, 2, *block), BF16),
            pltpu.VMEM((2, 4, 2, *block), BF16),
            pltpu.VMEM((8, 8, 128), F32),
            pltpu.VMEM((8, 8, 128), F32),
            pltpu.VMEM(block, F32),
            pltpu.VMEM((2, rows, 128), F32),
            pltpu.VMEM((2, rows, 128), F32),
            dma((6,)),
            dma((2, 4, 2, CUTS)),
            dma((2, 4, 2, CUTS)),
            dma((2, 4, 2, CUTS)),
            dma((2, 4, 2, CUTS)),
        ]
        + [dma((2, TILES, 2))] * 8
        + [dma((2,)), dma((2,)), dma((1,)), dma((1,))],
        compiler_params=pltpu.CompilerParams(
            collective_id=0, has_side_effects=True, vmem_limit_bytes=60 * 1024 * 1024
        ),
    )(tokens, group_ids, expert_ids, gate_weights, w_gate, w_up, w_down)


def solution(mesh):
    placed = (
        P(("group", "member"), "half"),
        P(("group", "member"), None),
        P(None, ("group", "member"), None),
        P(None, ("group", "member"), None),
        P(("group", "member"), None, "half"),
        P(("group", "member"), None, "half"),
        P(("group", "member"), "half", None),
    )
    return jax.shard_map(
        on_device,
        mesh=mesh,
        in_specs=placed,
        out_specs=P(("group", "member"), "half"),
        check_vma=False,
    )
```

```python
import jax
import jax.numpy as jnp
from jax import lax
from jax.experimental import pallas as pl
from jax.experimental.pallas import tpu as pltpu
from jax.sharding import PartitionSpec as P

MESH = pl.DeviceIdType.MESH
BF16 = jnp.bfloat16
F32 = jnp.float32
EPSILON = 1e-6
TILE = 8
TILES = 6
CUTS = 4
BLOCKS = 8
STEP_OF_BLOCK = (0, -1, 1, -2, 2, -3, 3, 4)
FILL = (
    ((1, 0, 0, 6), (0, 6, 6, 8)),
    ((2, 0, 0, 6), (0, 4, 6, 8)),
    ((3, 0, 0, 4), (4, 4, 4, 8)),
    ((5, 0, 0, 6), (3, 2, 6, 8)),
    ((6, 0, 0, 6), (4, 2, 6, 8)),
    ((7, 0, 0, 6), (0, 2, 6, 8)),
)
HALVED = 3
KEPT = (
    (0, 1, 2, 3), (0, 1, 2, 3), (0, 1, 2, 3),
    (0, 2, 1, 3), (1, 3, 0, 2), (0, 1, 2, 3),
)
FAR = ((0, 2), (1, 3))
NEAR = ((1, 3), (0, 2))


PLAN = (
    ("GO", 0, 0), ("MC", 0, 0), ("M", 0, 0), ("G", 1, 0), ("G", 1, 1), ("G", 1, 2), ("G", 1, 3), ("C", 1, 0),
    ("G", 2, 1), ("C", 0, 0), ("G", 2, 0), ("G", 2, 2), ("G", 2, 3), ("C", 2, 0), ("G", 3, 1), ("G", 3, 0),
    ("C", 4, 0), ("G", 3, 2), ("L", 0, 0), ("C", 3, 0), ("G", 3, 3), ("C", 4, 1), ("L", 1, 0), ("C", 3, 1),
    ("X", 0, 0), ("G", 4, 1), ("L", 4, 0), ("G", 4, 0), ("C", 5, 0), ("L", 4, 1), ("C", 5, 1), ("L", 3, 0),
    ("L", 3, 1), ("X", 4, 0), ("X", 3, 0), ("B", 4, 0), ("L", 5, 0), ("B", 3, 0), ("L", 5, 1), ("L", 2, 0),
    ("B", 4, 1), ("X", 5, 0), ("X", 2, 0), ("B", 5, 0), ("B", 5, 1), ("T", 4, 0), ("W", 6, 0), ("T", 3, 0),
    ("W", 5, 0), ("R", 1, 3), ("B", 3, 1), ("R", 1, 2), ("X", 1, 0), ("T", 4, 1), ("B", 2, 0), ("T", 5, 0),
    ("W", 7, 0), ("R", 0, 0), ("T", 5, 1), ("W", 7, 1), ("R", 0, 1), ("B", 1, 0), ("T", 3, 1), ("B", 0, 0),
    ("W", 6, 1), ("W", 5, 1), ("R", 1, 0), ("R", 1, 1), ("T", 2, 0), ("W", 3, 0), ("W", 4, 0), ("R", 2, 2),
    ("R", 2, 3), ("T", 1, 0), ("R", 2, 1), ("R", 2, 0), ("W", 2, 0), ("T", 0, 0), ("W", 1, 0), ("R", 3, 3),
    ("R", 3, 1), ("R", 3, 0), ("R", 3, 2), ("W", 0, 0), ("F1", 0, 0), ("F2", 0, 0),
)


def turned_dot(left, right):
    return lax.dot_general(left, right, (((0,), (0,)), ((), ())), preferred_element_type=F32)


def kernel(
    tok_ref, gid_ref, eid_ref, gw_ref, wg_hbm, wu_hbm, wd_hbm, out_ref,
    wg, wu, wd, xa, sel, rows_in, part_out, part_in, acc, term_out, term_in, yv, ring_out, ring_in,
    meta_out, meta, lift, sq_out, sq_in,
    w_sem, g_send, g_recv, r_send, r_recv, x_send, x_recv, t_send, t_recv, d_send, d_recv, p_send, p_recv,
    n_send, n_recv, m_send, m_recv,
):
    g = lax.axis_index("group")
    m = lax.axis_index("member")
    h = lax.axis_index("half")
    groups, members = 16, 8
    rows, width = tok_ref.shape
    cut = width // CUTS

    def place(group=None, member=None, half=None):
        return (
            g if group is None else group,
            m if member is None else member,
            h if half is None else half,
        )

    above = place(member=lax.rem(m + 1, members))
    below = place(member=lax.rem(m + members - 1, members))
    sibling = place(half=1 - h)
    ring_to = (above, below)

    def send(src, dst, send_sem, recv_sem, target):
        return pltpu.make_async_remote_copy(
            src_ref=src, dst_ref=dst, send_sem=send_sem, recv_sem=recv_sem,
            device_id=target, device_id_type=MESH,
        )

    barrier = pltpu.get_barrier_semaphore()

    def greet(target):
        pl.semaphore_signal(barrier, inc=1, device_id=target, device_id_type=MESH)

    greet(sibling)

    def greet_member(d, c):
        greet(place(member=lax.rem(m + d, members)))
        return c

    def greet_group(d, c):
        greet(place(group=lax.rem(g + d, groups)))
        return c

    lax.fori_loop(1, members, greet_member, 0)
    lax.fori_loop(1, groups, greet_group, 0)

    own_k = pl.ds(pl.multiple_of(h * width, width), width)
    other_k = pl.ds(pl.multiple_of((1 - h) * width, width), width)
    weight_copies = [
        pltpu.make_async_copy(wg_hbm.at[0, own_k, :], wg.at[0], w_sem.at[0]),
        pltpu.make_async_copy(wg_hbm.at[0, other_k, :], wg.at[1], w_sem.at[1]),
        pltpu.make_async_copy(wu_hbm.at[0, own_k, :], wu.at[0], w_sem.at[2]),
        pltpu.make_async_copy(wu_hbm.at[0, other_k, :], wu.at[1], w_sem.at[3]),
        pltpu.make_async_copy(wd_hbm.at[0, :, own_k], wd.at[0], w_sem.at[4]),
        pltpu.make_async_copy(wd_hbm.at[0, :, other_k], wd.at[1], w_sem.at[5]),
    ]
    for copy in weight_copies:
        copy.start()

    down = lax.broadcasted_iota(jnp.int32, (rows, rows), 0)


    def lanes(c):
        return pl.ds(c * cut, cut)

    def g_copy(p, step, way, c):
        src = 0 if step == 1 else 2 * step - 3 + way
        dst = 7 if step == 4 else 2 * step - 1 + way
        return send(
            xa.at[p, src, c], xa.at[p, dst, c],
            g_send.at[p, step - 1, way, c], g_recv.at[p, step - 1, way, c], ring_to[way],
        )

    def gather_start(p):
        for i in range(CUTS):
            for way in (0, 1):
                g_copy(p, 1, way, (FAR[way] + NEAR[way])[i]).start()

    def gather(p, step, which):
        for i in which:
            for way in (0, 1):
                c = (FAR[way] + NEAR[way])[i]
                g_copy(p, step, way, c).wait_recv()
                if step < 3 or (step == 3 and i < 2):
                    g_copy(p, step + 1, way, c).start()

    def matches(p, k, filling):
        j, off, low, high = filling
        record = meta[lax.rem(m + members + STEP_OF_BLOCK[j], members)]
        code = record[p : p + 1, :].astype(jnp.int32)
        gate = record[2 + p : 3 + p, :]
        at = (code & 7) + off
        good = (code >= 0) & (at >= low) & (at < high)
        return down == jnp.where(good, code + off, -1), gate

    def parts_of(k):
        return (0, 1) if k >= HALVED else (None,)

    def cuts_of(f):
        return range(CUTS) if f is None else range(2 * f, 2 * f + 2)

    def sem_of(f):
        return 0 if f is None else f

    def piece(ref, f):
        return ref if f is None else ref.at[pl.ds(2 * f, 2)]

    def pieces(ref, f):
        return ref if f is None else ref.at[:, pl.ds(2 * f, 2)]

    def choose(p, k, f=None):
        picks = []
        for filling in FILL[k]:
            hit, _ = matches(p, k, filling)
            picks.append((jnp.where(hit, 1.0, 0.0).astype(BF16), filling[0]))
        for i in cuts_of(f):
            total = sum(
                jnp.dot(pick, xa[p, j, KEPT[k][i]], preferred_element_type=F32) for pick, j in picks
            )
            sel[p, k, :, i] = total.astype(BF16).reshape(groups, TILE, cut)
            rows_in[p, k, 0, pl.ds(g, 1), i] = sel[p, k, pl.ds(g, 1), i]

        def start(d, carry):
            t = lax.rem(g + d, groups)
            send(
                piece(sel.at[p, k, t], f), piece(rows_in.at[p, k, 0, g], f),
                x_send.at[p, k, sem_of(f)], x_recv.at[p, k, sem_of(f)], place(group=t),
            ).start()
            return carry

        lax.fori_loop(1, groups, start, 0)

    def most(ref, sem, f):
        part = ref.at[pl.ds(0, groups - 1)] if f is None else ref.at[pl.ds(0, groups - 1), pl.ds(2 * f, 2)]
        pltpu.make_async_copy(part, part, sem).wait()

    def row_copy(p, k, f=None):
        return send(
            pieces(rows_in.at[p, k, 0], f), pieces(rows_in.at[p, k, 1], f),
            d_send.at[p, k, sem_of(f)], d_recv.at[p, k, sem_of(f)], sibling,
        )

    def landed(p, k, f=None):
        most(rows_in.at[p, k, 0], x_recv.at[p, k, sem_of(f)], f)
        row_copy(p, k, f).start()

    def part_copy(p, k, f=None):
        return send(
            piece(part_out.at[p, k], f), piece(part_in.at[p, k], f),
            p_send.at[p, k, sem_of(f)], p_recv.at[p, k, sem_of(f)], sibling,
        )

    def expert(p, k):
        pre = jnp.zeros((rows, wg.shape[2]), F32)
        up = jnp.zeros((rows, wg.shape[2]), F32)
        for side in (0, 1):
            for f in parts_of(k):
                if side == 1:
                    row_copy(p, k, f).wait_recv()
                for i in cuts_of(f):
                    some = rows_in[p, k, side, :, i].reshape(rows, cut)
                    pre += jnp.dot(some, wg[side, lanes(KEPT[k][i]), :], preferred_element_type=F32)
                    up += jnp.dot(some, wu[side, lanes(KEPT[k][i]), :], preferred_element_type=F32)
        hidden = (jax.nn.silu(pre) * up).astype(BF16)
        for f in parts_of(k):
            for i in cuts_of(f):
                part_out[p, k, i] = jnp.dot(
                    hidden, wd[1, :, lanes(KEPT[k][i])], preferred_element_type=F32
                ).astype(BF16)
            part_copy(p, k, f).start()
        for i in range(CUTS):
            acc[k, i] = jnp.dot(hidden, wd[0, :, lanes(KEPT[k][i])], preferred_element_type=F32)

    def give_back(p, k, f=None):
        part_copy(p, k, f).wait_recv()
        for c in cuts_of(f):
            total = acc[k, c] + part_in[p, k, c].astype(F32)
            term_out[p, k, :, c] = total.astype(BF16).reshape(groups, TILE, cut)
            term_in[p, k, pl.ds(g, 1), c] = term_out[p, k, pl.ds(g, 1), c]

        def start(d, carry):
            t = lax.rem(g + d, groups)
            send(
                piece(term_out.at[p, k, t], f), piece(term_in.at[p, k, g], f),
                t_send.at[p, k, sem_of(f)], t_recv.at[p, k, sem_of(f)], place(group=t),
            ).start()
            return carry

        lax.fori_loop(1, groups, start, 0)

    def returned(p, k, f=None):
        most(term_in.at[p, k], t_recv.at[p, k, sem_of(f)], f)

    def weigh(p, j, f=None):
        picks = []
        for k in range(TILES):
            for filling in FILL[k]:
                if filling[0] == j:
                    hit, gate = matches(p, k, filling)
                    picks.append((jnp.where(hit, gate, 0.0).astype(BF16), k))
        some = range(CUTS) if f is None else [KEPT[picks[0][1]][i] for i in cuts_of(f)]
        for c in some:
            yv[j, c] = sum(
                turned_dot(pick, term_in[p, k, :, KEPT[k].index(c)].reshape(rows, cut))
                for pick, k in picks
            )

    def r_copy(p, msg, way, c):
        return send(
            ring_out.at[p, msg, way, c], ring_in.at[p, msg, way, c],
            r_send.at[p, msg, way, c], r_recv.at[p, msg, way, c], ring_to[way],
        )

    def pass_on(p, msg, way, c, add):
        value = yv[7 if msg == 0 else 8 - 2 * msg - way, c]
        if add:
            r_copy(p, msg - 1, way, c).wait_recv()
            value += ring_in[p, msg - 1, way, c].astype(F32)
        ring_out[p, msg, way, c] = value.astype(BF16)
        r_copy(p, msg, way, c).start()

    def sums(p, msg, u):
        for way in (0, 1):
            pass_on(p, msg, way, (FAR[way] + NEAR[way])[u], msg > 1 or (msg == 1 and u < 2))

    def square_copy(p):
        return send(sq_out.at[p], sq_in.at[p], n_send.at[p], n_recv.at[p], sibling)

    def finish(p):
        squares = jnp.zeros((rows, 128), F32)
        for c in (0, 1, 2, 3):
            value = xa[p, 0, c].astype(F32) + yv[0, c]
            for way in (0, 1):
                r_copy(p, 3, way, c).wait_recv()
                value += ring_in[p, 3, way, c].astype(F32)
            lift[c] = value
            square = value * value
            for i in range(0, cut, 128):
                squares += square[:, i : i + 128]
        sq_out[p] = squares
        square_copy(p).start()

    def norm(p):
        square_copy(p).wait_recv()
        mean = jnp.sum(sq_out[p] + sq_in[p], axis=1, keepdims=True) / (2 * width)
        scale = lax.rsqrt(mean + EPSILON)
        for c in range(CUTS):
            value = (lift[c] * scale).astype(BF16)
            if p == 0:
                xa[1, 0, c] = value
            else:
                out_ref[:, lanes(c)] = value

    for c in range(CUTS):
        xa[0, 0, c] = tok_ref[:, lanes(c)]
    pl.semaphore_wait(barrier, groups + members - 1)
    gather_start(0)

    def make_meta():
        lane = lax.broadcasted_iota(jnp.int32, (rows, rows), 1)
        number = lax.broadcasted_iota(jnp.int32, (groups, rows), 0)
        group_of = gid_ref[...]
        onehot = jnp.where(number == group_of, 1.0, 0.0).astype(BF16)
        before = jnp.where(down < lane, turned_dot(onehot, onehot), 0.0).astype(BF16)
        meta_out[...] = jnp.zeros_like(meta_out)
        for p in (0, 1):
            ids = eid_ref[p]
            weights = gw_ref[p].astype(F32)
            named = jnp.zeros((groups, rows), F32)
            gates = jnp.zeros((groups, rows), F32)
            for c in range(ids.shape[0]):
                hit = number == ids[c : c + 1]
                named += jnp.where(hit, 1.0, 0.0)
                gates += jnp.where(hit, weights[c : c + 1], 0.0)
            rank = jnp.dot(named.astype(BF16), before, preferred_element_type=F32)
            code = jnp.where(named > 0.5, group_of.astype(F32) * TILE + rank, -1.0)
            for e in range(members):
                meta_out[e, p : p + 1, :] = code[e : e + 1]
                meta_out[e, 2 + p : 3 + p, :] = gates[e : e + 1]
        meta[pl.ds(m, 1)] = meta_out[pl.ds(m, 1)]

        def send_meta(d, c):
            to = lax.rem(m + d, members)
            send(meta_out.at[to], meta.at[m], m_send.at[0], m_recv.at[0], place(member=to)).start()
            return c

        lax.fori_loop(1, members, send_meta, 0)

    def meta_wait(sem):
        part = meta.at[pl.ds(0, members - 1)]
        pltpu.make_async_copy(part, part, sem.at[0]).wait()

    def run(p, name, i, f):
        part = f if i >= HALVED else None
        if name == "GO":
            gather_start(p)
        elif name == "MC":
            make_meta()
        elif name == "M":
            meta_wait(m_recv)
        elif name == "G":
            gather(p, i, (f,))
        elif name == "C":
            choose(p, i, part)
        elif name == "L":
            landed(p, i, part)
        elif name == "X":
            expert(p, i)
        elif name == "B":
            give_back(p, i, part)
        elif name == "T":
            returned(p, i, part)
        elif name == "W":
            weigh(p, i, f if i > 4 else None)
        elif name == "R":
            sums(p, i, f)
        elif name == "F1":
            finish(p)
        elif name == "F2":
            norm(p)

    for p in (0, 1):
        waited = p == 1
        for name, i, f in PLAN:
            if p == 0 and name == "GO" or p == 1 and name in ("MC", "M"):
                continue
            if name == "X" and not waited:
                waited = True
                for copy in weight_copies:
                    copy.wait()
            run(p, name, i, f)

    meta_wait(m_send)
    for p in (0, 1):
        square_copy(p).wait_send()
        for k in range(TILES):
            for f in parts_of(k):
                most(sel.at[p, k], x_send.at[p, k, sem_of(f)], f)
                most(term_out.at[p, k], t_send.at[p, k, sem_of(f)], f)
                row_copy(p, k, f).wait_send()
                part_copy(p, k, f).wait_send()
        for i in range(4):
            for way in (0, 1):
                for c in range(CUTS):
                    if i < 3 or c in FAR[way]:
                        g_copy(p, i + 1, way, c).wait_send()
                        r_copy(p, 3 - i, way, c).wait_send()


def on_device(tokens, group_ids, expert_ids, gate_weights, w_gate, w_up, w_down):
    rows, width = tokens.shape
    hidden = w_gate.shape[2]
    cut = width // CUTS
    tile = (16, CUTS, TILE, cut)
    block = (CUTS, rows, cut)
    vmem = pl.BlockSpec(memory_space=pltpu.VMEM)
    anywhere = pl.BlockSpec(memory_space=pl.ANY)
    dma = pltpu.SemaphoreType.DMA
    return pl.pallas_call(
        kernel,
        out_shape=jax.ShapeDtypeStruct((rows, width), BF16),
        in_specs=[vmem] * 4 + [anywhere] * 3,
        out_specs=vmem,
        scratch_shapes=[
            pltpu.VMEM((2, width, hidden), BF16),
            pltpu.VMEM((2, width, hidden), BF16),
            pltpu.VMEM((2, hidden, width), BF16),
            pltpu.VMEM((2, BLOCKS, *block), BF16),
            pltpu.VMEM((2, TILES, *tile), BF16),
            pltpu.VMEM((2, TILES, 2, *tile), BF16),
            pltpu.VMEM((2, TILES, *block), BF16),
            pltpu.VMEM((2, TILES, *block), BF16),
            pltpu.VMEM((TILES, *block), F32),
            pltpu.VMEM((2, TILES, *tile), BF16),
            pltpu.VMEM((2, TILES, *tile), BF16),
            pltpu.VMEM((BLOCKS, *block), F32),
            pltpu.VMEM((2, 4, 2, *block), BF16),
            pltpu.VMEM((2, 4, 2, *block), BF16),
            pltpu.VMEM((8, 8, 128), F32),
            pltpu.VMEM((8, 8, 128), F32),
            pltpu.VMEM(block, F32),
            pltpu.VMEM((2, rows, 128), F32),
            pltpu.VMEM((2, rows, 128), F32),
            dma((6,)),
            dma((2, 4, 2, CUTS)),
            dma((2, 4, 2, CUTS)),
            dma((2, 4, 2, CUTS)),
            dma((2, 4, 2, CUTS)),
        ]
        + [dma((2, TILES, 2))] * 8
        + [dma((2,)), dma((2,)), dma((1,)), dma((1,))],
        compiler_params=pltpu.CompilerParams(
            collective_id=0, has_side_effects=True, vmem_limit_bytes=60 * 1024 * 1024
        ),
    )(tokens, group_ids.T, jnp.swapaxes(expert_ids, 1, 2), jnp.swapaxes(gate_weights, 1, 2), w_gate, w_up, w_down)


def solution(mesh):
    placed = (
        P(("group", "member"), "half"),
        P(("group", "member"), None),
        P(None, ("group", "member"), None),
        P(None, ("group", "member"), None),
        P(("group", "member"), None, "half"),
        P(("group", "member"), None, "half"),
        P(("group", "member"), "half", None),
    )
    return jax.shard_map(
        on_device,
        mesh=mesh,
        in_specs=placed,
        out_specs=P(("group", "member"), "half"),
        check_vma=False,
    )
```

```python
import jax
import jax.numpy as jnp
from jax import lax
from jax.experimental import pallas as pl
from jax.experimental.pallas import tpu as pltpu
from jax.sharding import PartitionSpec as P

MESH = pl.DeviceIdType.MESH
BF16 = jnp.bfloat16
F32 = jnp.float32
EPSILON = 1e-6
TILE = 8
TILES = 6
CUTS = 4
BLOCKS = 8
STEP_OF_BLOCK = (0, -1, 1, -2, 2, -3, 3, 4)
FILL = (
    ((1, 0, 0, 6), (0, 6, 6, 8)),
    ((2, 0, 0, 6), (0, 4, 6, 8)),
    ((3, 0, 0, 4), (4, 4, 4, 8)),
    ((5, 0, 0, 6), (3, 2, 6, 8)),
    ((6, 0, 0, 6), (4, 2, 6, 8)),
    ((7, 0, 0, 6), (0, 2, 6, 8)),
)
HALVED = 3
KEPT = (
    (0, 1, 2, 3), (0, 1, 2, 3), (0, 1, 2, 3),
    (0, 2, 1, 3), (1, 3, 0, 2), (0, 1, 2, 3),
)
FAR = ((0, 2), (1, 3))
NEAR = ((1, 3), (0, 2))


PLAN = (
    ("GO", 0, 0), ("G", 1, 0), ("MC", 0, 0), ("G", 1, 1), ("G", 1, 2), ("M", 0, 0), ("G", 1, 3), ("C", 0, 0),
    ("G", 2, 0), ("C", 1, 0), ("G", 2, 1), ("G", 2, 2), ("G", 2, 3), ("C", 2, 0), ("G", 3, 1), ("G", 3, 0),
    ("C", 4, 0), ("G", 3, 2), ("C", 3, 0), ("G", 3, 3), ("C", 4, 1), ("C", 3, 1), ("L", 2, 0), ("L", 0, 0),
    ("G", 4, 1), ("C", 5, 1), ("X", 2, 0), ("G", 4, 0), ("L", 1, 0), ("L", 4, 0), ("L", 3, 0), ("C", 5, 0),
    ("B", 2, 0), ("L", 4, 1), ("L", 3, 1), ("X", 4, 0), ("X", 3, 0), ("B", 4, 0), ("L", 5, 0), ("B", 3, 0),
    ("L", 5, 1), ("B", 3, 1), ("X", 5, 0), ("X", 0, 0), ("B", 5, 1), ("B", 5, 0), ("T", 4, 0), ("W", 6, 0),
    ("T", 3, 0), ("W", 5, 0), ("R", 1, 3), ("T", 2, 0), ("B", 4, 1), ("R", 1, 2), ("T", 3, 1), ("X", 1, 0),
    ("T", 5, 1), ("W", 5, 1), ("W", 7, 1), ("R", 0, 1), ("W", 3, 0), ("B", 1, 0), ("T", 5, 0), ("W", 7, 0),
    ("R", 0, 0), ("T", 4, 1), ("W", 4, 0), ("R", 2, 2), ("B", 0, 0), ("W", 6, 1), ("R", 1, 1), ("R", 1, 0),
    ("R", 2, 3), ("T", 1, 0), ("R", 2, 1), ("T", 0, 0), ("W", 0, 0), ("R", 2, 0), ("W", 2, 0), ("W", 1, 0),
    ("R", 3, 2), ("R", 3, 3), ("R", 3, 0), ("R", 3, 1), ("F1", 0, 0), ("F2", 0, 0),
)


def turned_dot(left, right):
    return lax.dot_general(left, right, (((0,), (0,)), ((), ())), preferred_element_type=F32)


def kernel(
    tok_hbm, gid_hbm, eid_hbm, gw_hbm, wg_hbm, wu_hbm, wd_hbm, out_hbm,
    gid_ref, eid_ref, gw_ref, out_ref,
    wg, wu, wd, xa, sel, rows_in, part_out, part_in, acc, term_out, term_in, yv, ring_out, ring_in,
    meta_out, meta, lift, sq_out, sq_in,
    a_sem, o_sem, w_sem, g_send, g_recv, r_send, r_recv, x_send, x_recv, t_send, t_recv, d_send, d_recv, p_send, p_recv,
    n_send, n_recv, m_send, m_recv,
):
    g = lax.axis_index("group")
    m = lax.axis_index("member")
    h = lax.axis_index("half")
    groups, members = 16, 8
    rows, width = tok_hbm.shape
    cut = width // CUTS

    def place(group=None, member=None, half=None):
        return (
            g if group is None else group,
            m if member is None else member,
            h if half is None else half,
        )

    above = place(member=lax.rem(m + 1, members))
    below = place(member=lax.rem(m + members - 1, members))
    sibling = place(half=1 - h)
    ring_to = (above, below)

    def send(src, dst, send_sem, recv_sem, target):
        return pltpu.make_async_remote_copy(
            src_ref=src, dst_ref=dst, send_sem=send_sem, recv_sem=recv_sem,
            device_id=target, device_id_type=MESH,
        )

    barrier = pltpu.get_barrier_semaphore()

    def greet(target):
        pl.semaphore_signal(barrier, inc=1, device_id=target, device_id_type=MESH)

    greet(sibling)

    def greet_member(d, c):
        greet(place(member=lax.rem(m + d, members)))
        return c

    def greet_group(d, c):
        greet(place(group=lax.rem(g + d, groups)))
        return c

    lax.fori_loop(1, members, greet_member, 0)
    lax.fori_loop(1, groups, greet_group, 0)

    row_copies = [
        pltpu.make_async_copy(tok_hbm.at[:, pl.ds(c * cut, cut)], xa.at[0, 0, c], a_sem.at[c])
        for c in range(CUTS)
    ]
    route_copies = [
        pltpu.make_async_copy(gid_hbm, gid_ref, a_sem.at[CUTS]),
        pltpu.make_async_copy(eid_hbm, eid_ref, a_sem.at[CUTS + 1]),
        pltpu.make_async_copy(gw_hbm, gw_ref, a_sem.at[CUTS + 2]),
    ]
    for copy in row_copies + route_copies:
        copy.start()
    own_k = pl.ds(pl.multiple_of(h * width, width), width)
    other_k = pl.ds(pl.multiple_of((1 - h) * width, width), width)
    weight_copies = [
        pltpu.make_async_copy(wg_hbm.at[0, own_k, :], wg.at[0], w_sem.at[0]),
        pltpu.make_async_copy(wg_hbm.at[0, other_k, :], wg.at[1], w_sem.at[1]),
        pltpu.make_async_copy(wu_hbm.at[0, own_k, :], wu.at[0], w_sem.at[2]),
        pltpu.make_async_copy(wu_hbm.at[0, other_k, :], wu.at[1], w_sem.at[3]),
        pltpu.make_async_copy(wd_hbm.at[0, :, own_k], wd.at[0], w_sem.at[4]),
        pltpu.make_async_copy(wd_hbm.at[0, :, other_k], wd.at[1], w_sem.at[5]),
    ]
    for copy in weight_copies:
        copy.start()

    down = lax.broadcasted_iota(jnp.int32, (rows, rows), 0)


    def lanes(c):
        return pl.ds(c * cut, cut)

    def g_copy(p, step, way, c):
        src = 0 if step == 1 else 2 * step - 3 + way
        dst = 7 if step == 4 else 2 * step - 1 + way
        return send(
            xa.at[p, src, c], xa.at[p, dst, c],
            g_send.at[p, step - 1, way, c], g_recv.at[p, step - 1, way, c], ring_to[way],
        )

    def gather_start(p):
        for i in range(CUTS):
            for way in (0, 1):
                g_copy(p, 1, way, (FAR[way] + NEAR[way])[i]).start()

    def gather(p, step, which):
        for i in which:
            for way in (0, 1):
                c = (FAR[way] + NEAR[way])[i]
                g_copy(p, step, way, c).wait_recv()
                if step < 3 or (step == 3 and i < 2):
                    g_copy(p, step + 1, way, c).start()

    def matches(p, k, filling):
        j, off, low, high = filling
        record = meta[lax.rem(m + members + STEP_OF_BLOCK[j], members)]
        code = record[p : p + 1, :].astype(jnp.int32)
        gate = record[2 + p : 3 + p, :]
        at = (code & 7) + off
        good = (code >= 0) & (at >= low) & (at < high)
        return down == jnp.where(good, code + off, -1), gate

    def parts_of(k):
        return (0, 1) if k >= HALVED else (None,)

    def cuts_of(f):
        return range(CUTS) if f is None else range(2 * f, 2 * f + 2)

    def sem_of(f):
        return 0 if f is None else f

    def piece(ref, f):
        return ref if f is None else ref.at[pl.ds(2 * f, 2)]

    def pieces(ref, f):
        return ref if f is None else ref.at[:, pl.ds(2 * f, 2)]

    def choose(p, k, f=None):
        picks = []
        for filling in FILL[k]:
            hit, _ = matches(p, k, filling)
            picks.append((jnp.where(hit, 1.0, 0.0).astype(BF16), filling[0]))
        for i in cuts_of(f):
            total = sum(
                jnp.dot(pick, xa[p, j, KEPT[k][i]], preferred_element_type=F32) for pick, j in picks
            )
            sel[p, k, :, i] = total.astype(BF16).reshape(groups, TILE, cut)
            rows_in[p, k, 0, pl.ds(g, 1), i] = sel[p, k, pl.ds(g, 1), i]

        def start(d, carry):
            t = lax.rem(g + d, groups)
            send(
                piece(sel.at[p, k, t], f), piece(rows_in.at[p, k, 0, g], f),
                x_send.at[p, k, sem_of(f)], x_recv.at[p, k, sem_of(f)], place(group=t),
            ).start()
            return carry

        lax.fori_loop(1, groups, start, 0)

    def most(ref, sem, f):
        part = ref.at[pl.ds(0, groups - 1)] if f is None else ref.at[pl.ds(0, groups - 1), pl.ds(2 * f, 2)]
        pltpu.make_async_copy(part, part, sem).wait()

    def row_copy(p, k, f=None):
        return send(
            pieces(rows_in.at[p, k, 0], f), pieces(rows_in.at[p, k, 1], f),
            d_send.at[p, k, sem_of(f)], d_recv.at[p, k, sem_of(f)], sibling,
        )

    def landed(p, k, f=None):
        most(rows_in.at[p, k, 0], x_recv.at[p, k, sem_of(f)], f)
        row_copy(p, k, f).start()

    def part_copy(p, k, f=None):
        return send(
            piece(part_out.at[p, k], f), piece(part_in.at[p, k], f),
            p_send.at[p, k, sem_of(f)], p_recv.at[p, k, sem_of(f)], sibling,
        )

    def expert(p, k):
        pre = jnp.zeros((rows, wg.shape[2]), F32)
        up = jnp.zeros((rows, wg.shape[2]), F32)
        for side in (0, 1):
            for f in parts_of(k):
                if side == 1:
                    row_copy(p, k, f).wait_recv()
                for i in cuts_of(f):
                    some = rows_in[p, k, side, :, i].reshape(rows, cut)
                    pre += jnp.dot(some, wg[side, lanes(KEPT[k][i]), :], preferred_element_type=F32)
                    up += jnp.dot(some, wu[side, lanes(KEPT[k][i]), :], preferred_element_type=F32)
        hidden = (jax.nn.silu(pre) * up).astype(BF16)
        for f in parts_of(k):
            for i in cuts_of(f):
                part_out[p, k, i] = jnp.dot(
                    hidden, wd[1, :, lanes(KEPT[k][i])], preferred_element_type=F32
                ).astype(BF16)
            part_copy(p, k, f).start()
        for i in range(CUTS):
            acc[k, i] = jnp.dot(hidden, wd[0, :, lanes(KEPT[k][i])], preferred_element_type=F32)

    def give_back(p, k, f=None):
        part_copy(p, k, f).wait_recv()
        for c in cuts_of(f):
            total = acc[k, c] + part_in[p, k, c].astype(F32)
            term_out[p, k, :, c] = total.astype(BF16).reshape(groups, TILE, cut)
            term_in[p, k, pl.ds(g, 1), c] = term_out[p, k, pl.ds(g, 1), c]

        def start(d, carry):
            t = lax.rem(g + d, groups)
            send(
                piece(term_out.at[p, k, t], f), piece(term_in.at[p, k, g], f),
                t_send.at[p, k, sem_of(f)], t_recv.at[p, k, sem_of(f)], place(group=t),
            ).start()
            return carry

        lax.fori_loop(1, groups, start, 0)

    def returned(p, k, f=None):
        most(term_in.at[p, k], t_recv.at[p, k, sem_of(f)], f)

    def weigh(p, j, f=None):
        picks = []
        for k in range(TILES):
            for filling in FILL[k]:
                if filling[0] == j:
                    hit, gate = matches(p, k, filling)
                    picks.append((jnp.where(hit, gate, 0.0).astype(BF16), k))
        some = range(CUTS) if f is None else [KEPT[picks[0][1]][i] for i in cuts_of(f)]
        for c in some:
            yv[j, c] = sum(
                turned_dot(pick, term_in[p, k, :, KEPT[k].index(c)].reshape(rows, cut))
                for pick, k in picks
            )

    def r_copy(p, msg, way, c):
        return send(
            ring_out.at[p, msg, way, c], ring_in.at[p, msg, way, c],
            r_send.at[p, msg, way, c], r_recv.at[p, msg, way, c], ring_to[way],
        )

    def pass_on(p, msg, way, c, add):
        value = yv[7 if msg == 0 else 8 - 2 * msg - way, c]
        if add:
            r_copy(p, msg - 1, way, c).wait_recv()
            value += ring_in[p, msg - 1, way, c].astype(F32)
        ring_out[p, msg, way, c] = value.astype(BF16)
        r_copy(p, msg, way, c).start()

    def sums(p, msg, u):
        for way in (0, 1):
            pass_on(p, msg, way, (FAR[way] + NEAR[way])[u], msg > 1 or (msg == 1 and u < 2))

    def square_copy(p):
        return send(sq_out.at[p], sq_in.at[p], n_send.at[p], n_recv.at[p], sibling)

    def finish(p):
        squares = jnp.zeros((rows, 128), F32)
        for c in (0, 1, 2, 3):
            value = xa[p, 0, c].astype(F32) + yv[0, c]
            for way in (0, 1):
                r_copy(p, 3, way, c).wait_recv()
                value += ring_in[p, 3, way, c].astype(F32)
            lift[c] = value
            square = value * value
            for i in range(0, cut, 128):
                squares += square[:, i : i + 128]
        sq_out[p] = squares
        square_copy(p).start()

    def out_copy(c):
        return pltpu.make_async_copy(out_ref.at[c], out_hbm.at[:, lanes(c)], o_sem.at[c])

    def norm(p):
        square_copy(p).wait_recv()
        mean = jnp.sum(sq_out[p] + sq_in[p], axis=1, keepdims=True) / (2 * width)
        scale = lax.rsqrt(mean + EPSILON)
        for c in range(CUTS):
            value = (lift[c] * scale).astype(BF16)
            if p == 0:
                xa[1, 0, c] = value
            else:
                out_ref[c] = value
                out_copy(c).start()

    for copy in row_copies:
        copy.wait()
    pl.semaphore_wait(barrier, groups + members - 1)
    gather_start(0)

    def make_meta():
        for copy in route_copies:
            copy.wait()
        lane = lax.broadcasted_iota(jnp.int32, (rows, rows), 1)
        number = lax.broadcasted_iota(jnp.int32, (groups, rows), 0)
        group_of = gid_ref[...]
        onehot = jnp.where(number == group_of, 1.0, 0.0).astype(BF16)
        before = jnp.where(down < lane, turned_dot(onehot, onehot), 0.0).astype(BF16)
        meta_out[...] = jnp.zeros_like(meta_out)
        for p in (0, 1):
            ids = eid_ref[p]
            weights = gw_ref[p].astype(F32)
            named = jnp.zeros((groups, rows), F32)
            gates = jnp.zeros((groups, rows), F32)
            for c in range(ids.shape[0]):
                hit = number == ids[c : c + 1]
                named += jnp.where(hit, 1.0, 0.0)
                gates += jnp.where(hit, weights[c : c + 1], 0.0)
            rank = jnp.dot(named.astype(BF16), before, preferred_element_type=F32)
            code = jnp.where(named > 0.5, group_of.astype(F32) * TILE + rank, -1.0)
            for e in range(members):
                meta_out[e, p : p + 1, :] = code[e : e + 1]
                meta_out[e, 2 + p : 3 + p, :] = gates[e : e + 1]
        meta[pl.ds(m, 1)] = meta_out[pl.ds(m, 1)]

        def send_meta(d, c):
            to = lax.rem(m + d, members)
            send(meta_out.at[to], meta.at[m], m_send.at[0], m_recv.at[0], place(member=to)).start()
            return c

        lax.fori_loop(1, members, send_meta, 0)

    def meta_wait(sem):
        part = meta.at[pl.ds(0, members - 1)]
        pltpu.make_async_copy(part, part, sem.at[0]).wait()

    def run(p, name, i, f):
        part = f if i >= HALVED else None
        if name == "GO":
            gather_start(p)
        elif name == "MC":
            make_meta()
        elif name == "M":
            meta_wait(m_recv)
        elif name == "G":
            gather(p, i, (f,))
        elif name == "C":
            choose(p, i, part)
        elif name == "L":
            landed(p, i, part)
        elif name == "X":
            expert(p, i)
        elif name == "B":
            give_back(p, i, part)
        elif name == "T":
            returned(p, i, part)
        elif name == "W":
            weigh(p, i, f if i > 4 else None)
        elif name == "R":
            sums(p, i, f)
        elif name == "F1":
            finish(p)
        elif name == "F2":
            norm(p)

    for p in (0, 1):
        waited = p == 1
        for name, i, f in PLAN:
            if p == 0 and name == "GO" or p == 1 and name in ("MC", "M"):
                continue
            if name == "X" and not waited:
                waited = True
                for copy in weight_copies:
                    copy.wait()
            run(p, name, i, f)

    meta_wait(m_send)
    for c in range(CUTS):
        out_copy(c).wait()
    for p in (0, 1):
        square_copy(p).wait_send()
        for k in range(TILES):
            for f in parts_of(k):
                most(sel.at[p, k], x_send.at[p, k, sem_of(f)], f)
                most(term_out.at[p, k], t_send.at[p, k, sem_of(f)], f)
                row_copy(p, k, f).wait_send()
                part_copy(p, k, f).wait_send()
        for i in range(4):
            for way in (0, 1):
                for c in range(CUTS):
                    if i < 3 or c in FAR[way]:
                        g_copy(p, i + 1, way, c).wait_send()
                        r_copy(p, 3 - i, way, c).wait_send()


def on_device(tokens, group_ids, expert_ids, gate_weights, w_gate, w_up, w_down):
    rows, width = tokens.shape
    hidden = w_gate.shape[2]
    cut = width // CUTS
    tile = (16, CUTS, TILE, cut)
    block = (CUTS, rows, cut)
    anywhere = pl.BlockSpec(memory_space=pl.ANY)
    dma = pltpu.SemaphoreType.DMA
    return pl.pallas_call(
        kernel,
        out_shape=jax.ShapeDtypeStruct((rows, width), BF16),
        in_specs=[anywhere] * 7,
        out_specs=anywhere,
        scratch_shapes=[
            pltpu.VMEM((1, rows), jnp.int32),
            pltpu.VMEM((2, 4, rows), jnp.int32),
            pltpu.VMEM((2, 4, rows), BF16),
            pltpu.VMEM(block, BF16),
            pltpu.VMEM((2, width, hidden), BF16),
            pltpu.VMEM((2, width, hidden), BF16),
            pltpu.VMEM((2, hidden, width), BF16),
            pltpu.VMEM((2, BLOCKS, *block), BF16),
            pltpu.VMEM((2, TILES, *tile), BF16),
            pltpu.VMEM((2, TILES, 2, *tile), BF16),
            pltpu.VMEM((2, TILES, *block), BF16),
            pltpu.VMEM((2, TILES, *block), BF16),
            pltpu.VMEM((TILES, *block), F32),
            pltpu.VMEM((2, TILES, *tile), BF16),
            pltpu.VMEM((2, TILES, *tile), BF16),
            pltpu.VMEM((BLOCKS, *block), F32),
            pltpu.VMEM((2, 4, 2, *block), BF16),
            pltpu.VMEM((2, 4, 2, *block), BF16),
            pltpu.VMEM((8, 8, 128), F32),
            pltpu.VMEM((8, 8, 128), F32),
            pltpu.VMEM(block, F32),
            pltpu.VMEM((2, rows, 128), F32),
            pltpu.VMEM((2, rows, 128), F32),
            dma((CUTS + 3,)),
            dma((CUTS,)),
            dma((6,)),
            dma((2, 4, 2, CUTS)),
            dma((2, 4, 2, CUTS)),
            dma((2, 4, 2, CUTS)),
            dma((2, 4, 2, CUTS)),
        ]
        + [dma((2, TILES, 2))] * 8
        + [dma((2,)), dma((2,)), dma((1,)), dma((1,))],
        compiler_params=pltpu.CompilerParams(
            collective_id=0, has_side_effects=True, vmem_limit_bytes=60 * 1024 * 1024
        ),
    )(tokens, group_ids.T, jnp.swapaxes(expert_ids, 1, 2), jnp.swapaxes(gate_weights, 1, 2), w_gate, w_up, w_down)


def solution(mesh):
    placed = (
        P(("group", "member"), "half"),
        P(("group", "member"), None),
        P(None, ("group", "member"), None),
        P(None, ("group", "member"), None),
        P(("group", "member"), None, "half"),
        P(("group", "member"), None, "half"),
        P(("group", "member"), "half", None),
    )
    return jax.shard_map(
        on_device,
        mesh=mesh,
        in_specs=placed,
        out_specs=P(("group", "member"), "half"),
        check_vma=False,
    )
```
